128 devices in a mesh: tm: 4 (over y), chan: 32 (over z, x, core).
Axes of the slice: x: 4, y: 4, z: 4, core: 2. Of those that a mesh axis runs over, the one named last changes fastest.
Arguments:
- raw_traces: float32 [8192, 32768], P(None, ('tm', 'chan'))
- fir_taps: float32 [129], replicated, may hold values from -0.5 to 0.5
- chan_order: int32 [8192], replicated, may hold values from 0 to 8191, each once
- vs_index: int32 [64], replicated, may hold values from 0 to 8191
Outputs:
- stacked: float32 [64, 8192, 1024], P('tm', 'chan')
The draws below stay inside these ranges and needn't reach their ends.
Inputs may be any that keep to these rules, and one draw needn't show every extreme that they name: `chan_order`: each of the 8192 positions names a different acquisition channel.
All inputs are finite; a program needn't handle non-finite values.
Results may differ from the reference program's by a relative error of at most 0.022.
Values may be sent and summed in bfloat16 or wider, within the bound.
A program may use at most 192 MiB of HBM per device.

```python
import math
import jax
import jax.numpy as jnp
from jax import lax

CB = 256
SEGS = 8
NF = 1024
NB = 128
K0 = 4
WS = 8
TAPS = 129
VS = 64
CH = 8192
T_ALL = 32768
N_TM = 4
N_CHAN = 32


def draw_raw_traces(key, part):
    noise_key = jax.random.fold_in(key, 101)
    rough_key = jax.random.fold_in(key, 202)
    gain_key = jax.random.fold_in(key, 303)
    times = jnp.arange(T_ALL, dtype=jnp.float32) / T_ALL
    base = jax.random.truncated_normal(noise_key, -4.0, 4.0, (CH, T_ALL), jnp.float32)
    ramp = jnp.exp(0.75 * times)
    rough = jnp.exp(jax.random.uniform(rough_key, (T_ALL // 128,), jnp.float32, 0.0, math.log(5.0)))
    envelope = ramp * jnp.repeat(rough, 128)
    gains = jnp.exp(jax.random.uniform(gain_key, (CH,), jnp.float32, 0.0, math.log(10.0)))
    return base * envelope[None, :] * gains[:, None]


def place_ends(entries, own_key, low, top_value):
    shape = entries.shape
    place = [jax.random.randint(jax.random.fold_in(own_key, axis), (), 0, shape[axis]) for axis in range(len(shape))]
    entries = entries.at[tuple(place)].set(low)
    longest = shape.index(max(shape))
    place[longest] = (place[longest] + 1) % shape[longest]
    return entries.at[tuple(place)].set(top_value)


def noise(own_key, shape, deviation, most, kind=jnp.bfloat16):
    drawn = jax.random.normal(own_key, shape, jnp.float32) * deviation
    return jnp.minimum(jnp.maximum(drawn, -most), most).astype(kind)


def setup_inputs(seed: int = 0) -> dict:
    keys = jax.random.split(jax.random.key(seed), 5)
    raw_traces = draw_raw_traces(jax.random.fold_in(keys[4], 71), 0)
    fir_taps = noise(keys[1], (TAPS,), TAPS ** -0.5, 0.5, jnp.float32)
    chan_order = jax.random.permutation(keys[2], CH).astype(jnp.int32)
    vs_index = place_ends(jax.random.randint(keys[3], (VS,), 0, CH), jax.random.fold_in(keys[3], 1), 0, CH - 1).astype(jnp.int32)
    return dict(raw_traces=raw_traces, fir_taps=fir_taps, chan_order=chan_order, vs_index=vs_index)


exact_mode = lax.Precision.HIGHEST

def transform_tables(length, band_bins, lowest_frequency):
    bin_index = jnp.arange(band_bins, dtype=jnp.int32)[:, None] + lowest_frequency
    sample_index = jnp.arange(length, dtype=jnp.int32)[None, :]
    phase_index = (bin_index * sample_index % length).astype(jnp.float32) * (2.0 * math.pi / length)
    forward = jnp.concatenate([jnp.cos(phase_index), -jnp.sin(phase_index)], 0) / math.sqrt(length)
    lag_phase = (bin_index * (sample_index - length // 2) % length).astype(jnp.float32) * (2.0 * math.pi / length)
    inverse = jnp.concatenate([jnp.cos(lag_phase), -jnp.sin(lag_phase)], 0)
    return (forward, inverse)

def smoothing(band_bins, reach):
    row_bins = jnp.arange(band_bins, dtype=jnp.int32)[:, None]
    col_bins = jnp.arange(band_bins, dtype=jnp.int32)[None, :]
    nearby = (jnp.abs(row_bins - col_bins) <= reach).astype(jnp.float32)
    return nearby / lax.optimization_barrier(jnp.sum(nearby, 1, keepdims=True))

def apply_filter(padded, fir_taps):
    block_width = fir_taps.shape[0] - 1
    rows_idx = jnp.arange(block_width, dtype=jnp.int32)[:, None]
    cols_idx = jnp.arange(2 * block_width, dtype=jnp.int32)[None, :]
    offset = cols_idx - rows_idx
    kernel = jnp.where((offset >= 0) & (offset <= block_width), fir_taps[jnp.clip(offset, 0, block_width)], jnp.zeros((), fir_taps.dtype))
    blocks = padded.reshape(padded.shape[0] // block_width, block_width, padded.shape[1])
    first_part = jnp.einsum('rm,bmc->brc', kernel[:, :block_width], blocks[:-1], precision=exact_mode)
    second = jnp.einsum('rm,bmc->brc', kernel[:, block_width:], blocks[1:], precision=exact_mode)
    return (first_part + second).reshape(-1, padded.shape[1])

def whiten(spectra, smoother):
    band_bins = smoother.shape[0]
    real_rows = spectra[:, :band_bins]
    imag_rows = spectra[:, band_bins:]
    power_bins = real_rows * real_rows + imag_rows * imag_rows
    smooth = jnp.einsum('jk,skc->sjc', smoother, power_bins, precision=exact_mode)
    level_mean = lax.optimization_barrier(jnp.mean(power_bins, axis=1, keepdims=True))
    scale_bins = 1.0 / jnp.sqrt(smooth + 0.1 * level_mean + 1e-06)
    result = jnp.concatenate([real_rows * scale_bins, imag_rows * scale_bins], 1).astype(jnp.bfloat16)
    return lax.optimization_barrier(result)

def cross_spectra(sources, channels):
    band_bins = sources.shape[-2] // 2
    src_real = sources[..., :band_bins, :].astype(jnp.float32)
    src_imag = sources[..., band_bins:, :].astype(jnp.float32)
    chan_real = channels[..., :band_bins, :].astype(jnp.float32)
    chan_imag = channels[..., band_bins:, :].astype(jnp.float32)
    layout_kind = '...yhz,...yhm->...zhm'
    real_part = jnp.einsum(layout_kind, src_real, chan_real) + jnp.einsum(layout_kind, src_imag, chan_imag)
    imag_part = jnp.einsum(layout_kind, src_real, chan_imag) - jnp.einsum(layout_kind, src_imag, chan_real)
    return jnp.concatenate([real_part, imag_part], axis=-2)

def reference(raw_traces, fir_taps, chan_order, vs_index):
    forward, inverse = transform_tables(NF, NB, K0)
    smoother = smoothing(NB, WS)
    half_window_width = (TAPS - 1) // 2
    sample_total = SEGS * N_TM * NF
    scale_out = 1.0 / math.sqrt(SEGS * N_TM * NB)

    def process(block_index):
        columns = lax.dynamic_slice_in_dim(chan_order, block_index * CB, CB)
        traces = jnp.transpose(jnp.take(raw_traces, columns, axis=0))
        padded = jnp.pad(traces, ((half_window_width, half_window_width), (0, 0)))
        filtered = apply_filter(padded, fir_taps)
        root_mean = jnp.sqrt(lax.optimization_barrier(jnp.sum(filtered * filtered, 0)) / sample_total + 1e-06)
        clipped = jnp.clip(filtered, -2.0 * root_mean, 2.0 * root_mean)
        segments = clipped.reshape(SEGS * N_TM, NF, CB)
        spectra = jnp.einsum('kn,snc->skc', forward, segments, precision=exact_mode)
        return whiten(spectra, smoother)
    whitened_spectrum = lax.map(process, jnp.arange(N_CHAN, dtype=jnp.int32))
    picked = whitened_spectrum[vs_index // CB, :, :, vs_index % CB]
    sources = jnp.transpose(picked, (1, 2, 0))
    src_spans = sources.reshape(N_TM, SEGS, 2 * NB, VS)

    def correlate(block_spectra):
        chan_spans = block_spectra.reshape(N_TM, SEGS, 2 * NB, CB)
        partial_value = lax.optimization_barrier(cross_spectra(src_spans, chan_spans).astype(jnp.bfloat16))
        stacked_sum = lax.optimization_barrier(jnp.sum(partial_value.astype(jnp.float32), 0))
        return jnp.einsum('vkc,kl->vcl', stacked_sum, inverse, precision=exact_mode) * scale_out
    out_blocks = lax.map(correlate, whitened_spectrum)
    return jnp.transpose(out_blocks, (1, 0, 2, 3)).reshape(VS, CH, NF)
```

```python
import functools
import math

import jax
import jax.numpy as jnp
import numpy as np
from jax import lax
from jax.experimental import pallas as pl
from jax.experimental.pallas import tpu as pltpu
from jax.sharding import PartitionSpec as P

NF = 1024
NB = 128
K0 = 4
WS = 8
TAPS = 129
SLAB = 256
NBLK = 32
NTM = 4
SEGS = 8
VS = 64
VPT = VS // NTM
HALF = 128
T_ALL = SLAB * NBLK * NTM
MIB = 1024 * 1024
MESH = pl.DeviceIdType.MESH
BF = jnp.bfloat16
F32 = jnp.float32


def tables():
    k = np.arange(NB, dtype=np.int64)[:, None] + K0
    n = np.arange(NF, dtype=np.int64)[None, :]
    ph = (k * n % NF) * (2.0 * math.pi / NF)
    fwd = np.concatenate([np.cos(ph), -np.sin(ph)], 0) / math.sqrt(NF)
    lag = (k * (n - NF // 2) % NF) * (2.0 * math.pi / NF)
    inv = np.concatenate([np.cos(lag), -np.sin(lag)], 0) / math.sqrt(SEGS * NTM * NB)
    near = np.abs(np.arange(NB)[:, None] - np.arange(NB)[None, :]) <= WS
    count = near.sum(1)
    grow = np.concatenate([near, np.ones((NB, NB))], 0)
    return (
        fwd.astype(np.float32),
        inv.astype(np.float32),
        grow.astype(np.float32),
        (1.0 / count).astype(np.float32),
    )


def nt(a, b):
    return lax.dot_general(a, b, (((1,), (1,)), ((), ())), preferred_element_type=F32)


def tn(a, b):
    return lax.dot_general(a, b, (((0,), (0,)), ((), ())), preferred_element_type=F32)


def nn(a, b):
    return jnp.dot(a, b, preferred_element_type=F32)


def gather_kernel(order, vs, raw, out, src, buf):
    d = pl.program_id(0)

    def body(g, carry):
        for u in range(16):
            r = g * 16 + u
            buf[pl.ds(r, 1), :] = raw[pl.ds(order[d * SLAB + r], 1), :]
        return carry

    lax.fori_loop(0, SLAB // 16, body, 0)
    out[0] = buf[...].astype(BF)

    @pl.when(d == 0)
    def _():
        def pick(g, carry):
            for u in range(16):
                r = g * 16 + u
                buf[pl.ds(r, 1), :] = raw[pl.ds(order[vs[r]], 1), :]
            return carry

        lax.fori_loop(0, VS // 16, pick, 0)
        src[...] = buf[:VS].astype(BF)


def gather(raw, order, vs):
    rows, cols = raw.shape
    return pl.pallas_call(
        gather_kernel,
        grid_spec=pltpu.PrefetchScalarGridSpec(
            num_scalar_prefetch=2,
            grid=(NBLK,),
            in_specs=[pl.BlockSpec((rows, cols), lambda d, o, v: (0, 0))],
            out_specs=[
                pl.BlockSpec((1, SLAB, cols), lambda d, o, v: (d, 0, 0)),
                pl.BlockSpec((VS, cols), lambda d, o, v: (0, 0)),
            ],
            scratch_shapes=[pltpu.VMEM((SLAB, cols), F32)],
        ),
        out_shape=[
            jax.ShapeDtypeStruct((NBLK, SLAB, cols), BF),
            jax.ShapeDtypeStruct((VS, cols), BF),
        ],
        compiler_params=pltpu.CompilerParams(vmem_limit_bytes=40 * MIB),
    )(order, vs, raw)


def spectra_kernel(
    send, srcs, taps, fwd, grow, rcol, rrow, z_out, s_out,
    recv, recvs, tt, ybuf, ysrc, pbuf, zp, sp_out, ebuf, esrc,
    a_send, a_recv, h_send, h_recv, e_send, e_recv, g_send, g_recv, l_sem,
):
    i = lax.axis_index("tm")
    c = lax.axis_index("chan")
    cz, cx, cc = c // 8, (c // 2) % 4, c % 2

    def at_shift(d, sign):
        z = lax.rem(cz + sign * (d // 8) + 4, 4)
        x = lax.rem(cx + sign * ((d // 2) % 4) + 4, 4)
        k = lax.rem(cc + d % 2, 2)
        return z * 8 + x * 2 + k

    barrier = pltpu.get_barrier_semaphore()

    def greet(d, carry):
        pl.semaphore_signal(barrier, inc=1, device_id=(i, at_shift(d, 1)), device_id_type=MESH)
        return carry

    lax.fori_loop(1, NBLK, greet, 0)
    for d in range(1, NTM):
        pl.semaphore_signal(
            barrier, inc=1, device_id=(lax.rem(i + d, NTM), c), device_id_type=MESH
        )
    pl.semaphore_wait(barrier, NBLK - 1 + NTM - 1)

    def a2a(q, d, sign):
        other = at_shift(d, sign)
        if q == 2:
            src, dst = srcs, recvs.at[1 + c]
            land = recvs.at[1 + other]
        else:
            src = send.at[other, pl.ds(q * HALF, HALF)]
            dst = recv.at[q, 1 + c]
            land = recv.at[q, 1 + other]
        if sign > 0:
            return pltpu.make_async_remote_copy(
                src_ref=src, dst_ref=dst, send_sem=a_send.at[q, d], recv_sem=a_recv.at[q, c],
                device_id=(i, other), device_id_type=MESH,
            )
        return pltpu.make_async_remote_copy(
            src_ref=src, dst_ref=land, send_sem=a_send.at[q, d], recv_sem=a_recv.at[q, other],
            device_id=(i, other), device_id_type=MESH,
        )

    def own(q):
        if q == 2:
            return pltpu.make_async_copy(srcs, recvs.at[1 + c], l_sem.at[q])
        return pltpu.make_async_copy(
            send.at[c, pl.ds(q * HALF, HALF)], recv.at[q, 1 + c], l_sem.at[q]
        )

    for q in (2, 0, 1):
        own(q).start()

        def start(d, carry, q=q):
            a2a(q, d, 1).start()
            return carry

        lax.fori_loop(1, NBLK, start, 0)

    band = jnp.broadcast_to(taps[0:1, :], (SLAB, 2 * SLAB))
    tt[...] = pltpu.roll(band, 0, 1, stride=1, stride_axis=0).astype(BF)

    def box(q):
        return recvs if q == 2 else recv.at[q]

    def halo(q, side):
        b = box(q)
        if side == 0:
            return pltpu.make_async_remote_copy(
                src_ref=b.at[NBLK, :, pl.ds(128, 128)], dst_ref=b.at[0, :, pl.ds(128, 128)],
                send_sem=h_send.at[q, 0], recv_sem=h_recv.at[q, 0],
                device_id=(lax.rem(i + 1, NTM), c), device_id_type=MESH,
            )
        return pltpu.make_async_remote_copy(
            src_ref=b.at[1, :, pl.ds(0, 128)], dst_ref=b.at[NBLK + 1, :, pl.ds(0, 128)],
            send_sem=h_send.at[q, 1], recv_sem=h_recv.at[q, 1],
            device_id=(lax.rem(i + NTM - 1, NTM), c), device_id_type=MESH,
        )

    def arrive(q):
        own(q).wait()

        def wait(d, carry):
            a2a(q, d, -1).wait_recv()
            return carry

        lax.fori_loop(1, NBLK, wait, 0)
        b = box(q)
        rows = VS if q == 2 else HALF

        @pl.when(i < NTM - 1)
        def _():
            halo(q, 0).start()

        @pl.when(i > 0)
        def _():
            halo(q, 1).start()

        @pl.when(i == 0)
        def _():
            b[0, :, pl.ds(128, 128)] = jnp.zeros((rows, 128), BF)

        @pl.when(i == NTM - 1)
        def _():
            b[NBLK + 1, :, pl.ds(0, 128)] = jnp.zeros((rows, 128), BF)

    def halos_in(q):
        @pl.when(i > 0)
        def _():
            halo(q, 0).wait_recv()

        @pl.when(i < NTM - 1)
        def _():
            halo(q, 1).wait_recv()

    def energy_box(q):
        return esrc if q == 2 else ebuf.at[q]

    def energy(q, d):
        other = lax.rem(i + d, NTM)
        e = energy_box(q)
        return pltpu.make_async_remote_copy(
            src_ref=e.at[i], dst_ref=e.at[i], send_sem=e_send.at[q, d], recv_sem=e_recv.at[q, i],
            device_id=(other, c), device_id_type=MESH,
        )

    def energy_in(q, d):
        other = lax.rem(i + d, NTM)
        e = energy_box(q)
        return pltpu.make_async_remote_copy(
            src_ref=e.at[other], dst_ref=e.at[other], send_sem=e_send.at[q, d],
            recv_sem=e_recv.at[q, other], device_id=(other, c), device_id_type=MESH,
        )

    def gathered(q, d, sign):
        other = lax.rem(i + d, NTM)
        slot = i if sign > 0 else other
        if q == 2:
            src = sp_out.at[:, pl.ds(other * VPT, VPT)]
            dst = s_out.at[slot]
        else:
            src = zp.at[q]
            dst = z_out.at[:, pl.ds(slot * 16, 16), pl.ds(q * HALF, HALF)]
        return pltpu.make_async_remote_copy(
            src_ref=src, dst_ref=dst, send_sem=g_send.at[q, d], recv_sem=g_recv.at[q, slot],
            device_id=(other, c), device_id_type=MESH,
        )

    def gathered_own(q):
        if q == 2:
            return pltpu.make_async_copy(
                sp_out.at[:, pl.ds(i * VPT, VPT)], s_out.at[i], l_sem.at[3 + q]
            )
        return pltpu.make_async_copy(
            zp.at[q], z_out.at[:, pl.ds(i * 16, 16), pl.ds(q * HALF, HALF)], l_sem.at[3 + q]
        )

    def send_all(q):
        gathered_own(q).start()
        for d in range(1, NTM):
            gathered(q, d, 1).start()

    def filter_sources():
        def body(g, acc):
            b = g * 8
            w = jnp.concatenate(
                [
                    recvs[pl.ds(b, 8), :, 128:].reshape(8 * VS, 128),
                    recvs[pl.ds(b + 1, 8)].reshape(8 * VS, SLAB),
                    recvs[pl.ds(b + 2, 8), :, :128].reshape(8 * VS, 128),
                ],
                1,
            )
            y = nt(w, tt[...])
            ysrc[pl.ds(b, 8)] = y.astype(BF).reshape(8, VS, SLAB)
            sq = y * y
            sq = sq[:, :128] + sq[:, 128:]
            return acc + jnp.sum(sq.reshape(8, VS, 128), 0)

        esrc[i] = lax.fori_loop(0, NBLK // 8, body, jnp.zeros((VS, 128), F32))
        for d in range(1, NTM):
            energy(2, d).start()

    def filter_channels(q):
        def body(b, acc):
            w = jnp.concatenate(
                [recv[q, b, :, 128:], recv[q, b + 1], recv[q, b + 2, :, :128]], 1
            )
            y = nt(tt[...], w)
            ybuf[q, b] = y.astype(BF)
            return acc + jnp.sum((y * y).reshape(SLAB // 8, 8, HALF), 0)

        ebuf[q, i] = lax.fori_loop(0, NBLK, body, jnp.zeros((8, HALF), F32))
        for d in range(1, NTM):
            energy(q, d).start()

    def limit(total):
        return 2.0 * jnp.sqrt(total / T_ALL + 1e-6)

    def whiten_sources():
        for d in range(1, NTM):
            energy_in(2, d).wait_recv()
        total = esrc[0] + esrc[1] + esrc[2] + esrc[3]
        top = limit(jnp.sum(total, 1, keepdims=True))

        def body(s, carry):
            parts = []
            for j in range(4):
                y = ysrc[s * 4 + j].astype(F32)
                parts.append(jnp.clip(y, -top, top).astype(BF))
            sp = nt(jnp.concatenate(parts, 1), fwd[...])
            re, im = sp[:, :NB], sp[:, NB:]
            g = nt((re * re + im * im).astype(BF), grow[...])
            scale = lax.rsqrt(g[:, :NB] * rrow[0:1, :] + g[:, NB:] * (0.1 / NB) + 1e-6)
            sp_out[s] = jnp.concatenate([re * scale, im * scale], 1).astype(BF)
            return carry

        lax.fori_loop(0, SEGS, body, 0)
        send_all(2)

    def whiten_channels(q):
        for d in range(1, NTM):
            energy_in(q, d).wait_recv()
        total = ebuf[q, 0] + ebuf[q, 1] + ebuf[q, 2] + ebuf[q, 3]
        top = limit(jnp.sum(total, 0, keepdims=True))

        def body(s, carry):
            y = ybuf[q, pl.ds(s * 4, 4)].reshape(NF, HALF).astype(F32)
            y = jnp.clip(y, -top, top).astype(BF)
            sp = nn(fwd[...], y)
            re, im = sp[:NB], sp[NB:]
            g = nn(grow[...], (re * re + im * im).astype(BF))
            scale = lax.rsqrt(g[:NB] * rcol[...] + g[NB:] * (0.1 / NB) + 1e-6)
            pbuf[pl.ds(s, NB, stride=16), :] = re * scale
            pbuf[pl.ds(8 + s, NB, stride=16), :] = im * scale
            return carry

        lax.fori_loop(0, SEGS, body, 0)
        zp[q] = pbuf[...].reshape(NB, 16, HALF).astype(BF)
        send_all(q)

    arrive(2)
    halos_in(2)
    filter_sources()
    arrive(0)
    whiten_sources()
    halos_in(0)
    filter_channels(0)
    whiten_channels(0)
    arrive(1)
    halos_in(1)
    filter_channels(1)
    whiten_channels(1)

    for q in range(3):
        gathered_own(q).wait()
        for d in range(1, NTM):
            gathered(q, d, 1).wait_send()
            gathered(q, d, -1).wait_recv()
            energy(q, d).wait_send()

        @pl.when(i < NTM - 1)
        def _():
            halo(q, 0).wait_send()

        @pl.when(i > 0)
        def _():
            halo(q, 1).wait_send()

        def sent(d, carry, q=q):
            a2a(q, d, 1).wait_send()
            return carry

        lax.fori_loop(1, NBLK, sent, 0)


def whitened_spectra(send, srcs, taps, fwd, grow, rcol, rrow):
    vm = pl.BlockSpec(memory_space=pltpu.VMEM)
    hb = pl.BlockSpec(memory_space=pl.ANY)
    dma = pltpu.SemaphoreType.DMA
    return pl.pallas_call(
        spectra_kernel,
        out_shape=[
            jax.ShapeDtypeStruct((NB, NTM * 16, SLAB), BF),
            jax.ShapeDtypeStruct((NTM, SEGS, VPT, 2 * NB), BF),
        ],
        in_specs=[hb, hb, vm, vm, vm, vm, vm],
        out_specs=[hb, hb],
        scratch_shapes=[
            pltpu.VMEM((2, NBLK + 2, HALF, SLAB), BF),
            pltpu.VMEM((NBLK + 2, VS, SLAB), BF),
            pltpu.VMEM((SLAB, 2 * SLAB), BF),
            pltpu.VMEM((2, NBLK, SLAB, HALF), BF),
            pltpu.VMEM((NBLK, VS, SLAB), BF),
            pltpu.VMEM((NB * 16, HALF), F32),
            pltpu.VMEM((2, NB, 16, HALF), BF),
            pltpu.VMEM((SEGS, VS, 2 * NB), BF),
            pltpu.VMEM((2, NTM, 8, HALF), F32),
            pltpu.VMEM((NTM, VS, 128), F32),
            dma((3, NBLK)), dma((3, NBLK)), dma((3, 2)), dma((3, 2)),
            dma((3, NTM)), dma((3, NTM)), dma((3, NTM)), dma((3, NTM)), dma((6,)),
        ],
        compiler_params=pltpu.CompilerParams(
            collective_id=0, has_side_effects=True, vmem_limit_bytes=48 * MIB
        ),
    )(send, srcs, taps, fwd, grow, rcol, rrow)


def lag_kernel(z, s, inv, out, smat, u, x):
    v = pl.program_id(1)

    @pl.when((pl.program_id(0) == 0) & (v == 0))
    def _():
        flat = s[...].reshape(NTM * SEGS * VPT, 2 * NB).astype(F32)
        smat[0] = flat[:, :NB]
        smat[1] = flat[:, NB:]
        for w in range(VPT):
            re = smat[0, pl.ds(w, NTM * SEGS, stride=VPT), :]
            im = smat[1, pl.ds(w, NTM * SEGS, stride=VPT), :]
            real, imag = [], []
            for t in range(NTM):
                r, m = re[t * SEGS : (t + 1) * SEGS], im[t * SEGS : (t + 1) * SEGS]
                real += [r, m]
                imag += [-m, r]
            both = jnp.concatenate(real + imag, 0).T
            u[pl.ds(2 * w * NB, NB), 0:64] = both[:, :64]
            u[pl.ds((2 * w + 1) * NB, NB), 0:64] = both[:, 64:]

    @pl.when(v == 0)
    def _():
        def body(g, carry):
            for j in range(8):
                k = g * 8 + j
                lhs = u[pl.ds(k, 2 * VPT, stride=NB), :][:, :64].astype(BF)
                x[pl.ds(k, 2 * VPT, stride=NB), :] = nn(lhs, z[k])
            return carry

        lax.fori_loop(0, NB // 8, body, 0)

    rows = x[pl.ds(pl.multiple_of(v * 2 * NB, 2 * NB), 2 * NB), :]
    out[0] = tn(rows.astype(BF), inv[...])


def lags(z, s, inv):
    return pl.pallas_call(
        lag_kernel,
        grid=(2, VPT),
        in_specs=[
            pl.BlockSpec((NB, NTM * 16, HALF), lambda q, v: (0, 0, q)),
            pl.BlockSpec((NTM, SEGS, VPT, 2 * NB), lambda q, v: (0, 0, 0, 0)),
            pl.BlockSpec((2 * NB, NF), lambda q, v: (0, 0)),
        ],
        out_specs=pl.BlockSpec((1, HALF, NF), lambda q, v: (v, q, 0)),
        out_shape=jax.ShapeDtypeStruct((VPT, SLAB, NF), F32),
        scratch_shapes=[
            pltpu.VMEM((2, NTM * SEGS * VPT, NB), F32),
            pltpu.VMEM((2 * VPT * NB, 128), F32),
            pltpu.VMEM((2 * VPT * NB, HALF), F32),
        ],
        compiler_params=pltpu.CompilerParams(vmem_limit_bytes=40 * MIB),
    )(z, s, inv)


def on_device(raw_traces, fir_taps, chan_order, vs_index):
    fwd, inv, grow, rcount = tables()
    send, srcs = gather(raw_traces, chan_order, vs_index)
    taps = jnp.zeros((8, 2 * SLAB), F32).at[:, 64 : 64 + TAPS].set(fir_taps[None, :])
    z, s = whitened_spectra(
        send, srcs, taps,
        jnp.asarray(fwd, BF), jnp.asarray(grow, BF),
        jnp.asarray(np.broadcast_to(rcount[:, None], (NB, HALF))),
        jnp.asarray(np.broadcast_to(rcount[None, :], (8, NB))),
    )
    return lags(z, s, jnp.asarray(inv, BF))


def solution(mesh):
    in_specs = (P(None, ("tm", "chan")), P(), P(), P())
    out_specs = P("tm", "chan", None)
    return jax.shard_map(
        on_device, mesh=mesh, in_specs=in_specs, out_specs=out_specs, check_vma=False
    )
```

```python
import functools
import math

import jax
import jax.numpy as jnp
import numpy as np
from jax import lax
from jax.experimental import pallas as pl
from jax.experimental.pallas import tpu as pltpu
from jax.sharding import PartitionSpec as P

NF = 1024
NB = 128
K0 = 4
WS = 8
TAPS = 129
SLAB = 256
NBLK = 32
NTM = 4
SEGS = 8
VS = 64
VPT = VS // NTM
HALF = 128
T_ALL = SLAB * NBLK * NTM
MIB = 1024 * 1024
MESH = pl.DeviceIdType.MESH
BF = jnp.bfloat16
F32 = jnp.float32


def tables():
    k = np.arange(NB, dtype=np.int64)[:, None] + K0
    n = np.arange(NF, dtype=np.int64)[None, :]
    ph = (k * n % NF) * (2.0 * math.pi / NF)
    fwd = np.concatenate([np.cos(ph), -np.sin(ph)], 0) / math.sqrt(NF)
    lag = (k * (n - NF // 2) % NF) * (2.0 * math.pi / NF)
    inv = np.concatenate([np.cos(lag), -np.sin(lag)], 0) / math.sqrt(SEGS * NTM * NB)
    near = np.abs(np.arange(NB)[:, None] - np.arange(NB)[None, :]) <= WS
    count = near.sum(1)
    grow = np.concatenate([near, np.ones((NB, NB))], 0)
    return (
        fwd.astype(np.float32),
        inv.astype(np.float32),
        grow.astype(np.float32),
        (1.0 / count).astype(np.float32),
    )


def nt(a, b):
    return lax.dot_general(a, b, (((1,), (1,)), ((), ())), preferred_element_type=F32)


def tn(a, b):
    return lax.dot_general(a, b, (((0,), (0,)), ((), ())), preferred_element_type=F32)


def nn(a, b):
    return jnp.dot(a, b, preferred_element_type=F32)


def spectra_kernel(
    order, vs, raw, taps, fwd, grow, rcol, rrow, xout,
    rows2, line, send, srcs, recv, recvs, tt, ybuf, ysrc, pbuf, zp, z, sp_out, sg, smat, u, x,
    ebuf, esrc, r_sem, a_send, a_recv, h_send, h_recv, e_send, e_recv, g_send, g_recv,
    s_send, s_recv,
):
    i = lax.axis_index("tm")
    c = lax.axis_index("chan")
    cz, cx, cc = c // 8, (c // 2) % 4, c % 2
    group, base = c % NTM, (c // NTM) * NTM
    up, down = lax.rem(i + 1, NTM), lax.rem(i + NTM - 1, NTM)

    def at_shift(d, sign):
        d = (d * 11) % NBLK
        z = lax.rem(cz + sign * (d // 8) + 4, 4)
        x = lax.rem(cx + sign * ((d // 2) % 4) + 4, 4)
        k = lax.rem(cc + d % 2, 2)
        return z * 8 + x * 2 + k

    def load(p):
        part = raw.shape[0] // 4
        r = pl.ds((p // 2) * part, part)
        return pltpu.make_async_copy(
            raw.at[r, pl.ds((p % 2) * 128, 128)], rows2.at[r, p % 2], r_sem.at[p]
        )

    for p in range(8):
        load(p).start()

    barrier = pltpu.get_barrier_semaphore()

    def greet(d, carry):
        pl.semaphore_signal(barrier, inc=1, device_id=(i, at_shift(d, 1)), device_id_type=MESH)
        return carry

    lax.fori_loop(1, NBLK, greet, 0)
    for d in range(1, NTM):
        pl.semaphore_signal(
            barrier, inc=1, device_id=(lax.rem(i + d, NTM), c), device_id_type=MESH
        )
    for t in range(NTM):

        @pl.when((i != t) | (group != i))
        def _():
            pl.semaphore_signal(barrier, inc=1, device_id=(t, base + i), device_id_type=MESH)

    band = jnp.broadcast_to(taps[0:1, :], (SLAB, 2 * SLAB))
    tt[...] = pltpu.roll(band, 0, 1, stride=1, stride_axis=0).astype(BF)

    for p in range(8):
        load(p).wait()
    peers = NBLK - 1 + NTM - 1 + NTM

    @pl.when(group == i)
    def _():
        pl.semaphore_wait(barrier, peers - 1)

    @pl.when(group != i)
    def _():
        pl.semaphore_wait(barrier, peers)

    def a2a(q, d, sign):
        other = at_shift(d, sign)
        owner = c if sign > 0 else other
        if q == 2:
            src, dst = srcs.at[pl.ds((other % NTM) * VPT, VPT)], recvs.at[1 + owner]
        else:
            src, dst = send.at[q, d], recv.at[q, 1 + owner]
        return pltpu.make_async_remote_copy(
            src_ref=src, dst_ref=dst, send_sem=a_send.at[q, d], recv_sem=a_recv.at[q, owner],
            device_id=(i, other), device_id_type=MESH,
        )

    def fetch(count, position):
        def body(g, carry):
            for t in range(64):
                r = g * 64 + t
                line[pl.ds(pl.multiple_of(2 * r, 2), 2), :] = rows2[position(r)]
            return carry

        lax.fori_loop(0, count // 64, body, 0)
        return [line[pl.ds(h, count, stride=2), :].astype(BF) for h in range(2)]

    lo, hi = fetch(VS, lambda r: order[vs[r]])
    srcs[:, 0:128] = lo
    srcs[:, 128:256] = hi

    def send_sources(d, carry):
        a2a(2, d, 1).start()
        return carry

    lax.fori_loop(1, NBLK, send_sources, 0)
    recvs[1 + c] = srcs[pl.ds(pl.multiple_of(group * VPT, VPT), VPT)]

    def send_channels(q):
        lo, hi = fetch(HALF, lambda r: order[c * SLAB + q * HALF + r])
        recv[q, 1 + c, :, 0:128] = lo
        recv[q, 1 + c, :, 128:256] = hi

        def body(d, carry):
            start = at_shift(d, 1) * SLAB + q * HALF
            lo, hi = fetch(HALF, lambda r: order[start + r])
            send[q, d, :, 0:128] = lo
            send[q, d, :, 128:256] = hi
            if q == 1:
                a2a(0, d, 1).wait_send()
            a2a(q, d, 1).start()
            return carry

        lax.fori_loop(1, NBLK, body, 0)

    def box(q):
        return recvs if q == 2 else recv.at[q]

    def halo(q, side):
        b = box(q)
        if side == 0:
            return pltpu.make_async_remote_copy(
                src_ref=b.at[NBLK, :, pl.ds(128, 128)], dst_ref=b.at[0, :, pl.ds(128, 128)],
                send_sem=h_send.at[q, 0], recv_sem=h_recv.at[q, 0],
                device_id=(up, c), device_id_type=MESH,
            )
        return pltpu.make_async_remote_copy(
            src_ref=b.at[1, :, pl.ds(0, 128)], dst_ref=b.at[NBLK + 1, :, pl.ds(0, 128)],
            send_sem=h_send.at[q, 1], recv_sem=h_recv.at[q, 1],
            device_id=(down, c), device_id_type=MESH,
        )

    def arrive(q):
        def wait(d, carry):
            a2a(q, d, -1).wait_recv()
            return carry

        lax.fori_loop(1, NBLK, wait, 0)
        b = box(q)
        rows = VPT if q == 2 else HALF

        @pl.when(i < NTM - 1)
        def _():
            halo(q, 0).start()

        @pl.when(i > 0)
        def _():
            halo(q, 1).start()

        @pl.when(i == 0)
        def _():
            b[0, :, pl.ds(128, 128)] = jnp.zeros((rows, 128), BF)

        @pl.when(i == NTM - 1)
        def _():
            b[NBLK + 1, :, pl.ds(0, 128)] = jnp.zeros((rows, 128), BF)

    def halos_in(q):
        @pl.when(i > 0)
        def _():
            halo(q, 0).wait_recv()

        @pl.when(i < NTM - 1)
        def _():
            halo(q, 1).wait_recv()

    def energy(q, d, sign):
        other = lax.rem(i + d, NTM)
        owner = i if sign > 0 else other
        e = esrc if q == 2 else ebuf.at[q]
        return pltpu.make_async_remote_copy(
            src_ref=e.at[owner], dst_ref=e.at[owner], send_sem=e_send.at[q, d],
            recv_sem=e_recv.at[q, owner], device_id=(other, c), device_id_type=MESH,
        )

    def block(q, h, owner):
        return z.at[pl.ds(h * 64, 64), pl.ds(owner * 16, 16), pl.ds(q * HALF, HALF)]

    def direct(q, h, way):
        return pltpu.make_async_remote_copy(
            src_ref=zp.at[q, pl.ds(h * 64, 64)], dst_ref=block(q, h, i),
            send_sem=g_send.at[q, h, way], recv_sem=g_recv.at[q, h, i],
            device_id=(up if way == 0 else down, c), device_id_type=MESH,
        )

    def forward(q, h):
        owner = down if h == 0 else up
        return pltpu.make_async_remote_copy(
            src_ref=block(q, h, owner), dst_ref=block(q, h, owner),
            send_sem=g_send.at[q, h, 2], recv_sem=g_recv.at[q, h, owner],
            device_id=(up if h == 0 else down, c), device_id_type=MESH,
        )

    def landed(q, h, owner):
        return pltpu.make_async_remote_copy(
            src_ref=block(q, h, owner), dst_ref=block(q, h, owner),
            send_sem=g_send.at[q, h, 2], recv_sem=g_recv.at[q, h, owner],
            device_id=(up, c), device_id_type=MESH,
        )

    def spread(q):
        for h in range(2):
            direct(q, h, h).start()
        for h in range(2):
            direct(q, h, 1 - h).start()
        z[:, pl.ds(pl.multiple_of(i * 16, 16), 16), q * HALF : (q + 1) * HALF] = zp[q]

    def pass_on(q):
        for h in range(2):
            landed(q, h, down if h == 0 else up).wait_recv()
            forward(q, h).start()

    def collect(q):
        for h in range(2):
            landed(q, h, up if h == 0 else down).wait_recv()
            landed(q, h, lax.rem(i + 2, NTM)).wait_recv()

    def filter_sources():
        w = jnp.concatenate(
            [
                recvs[0:NBLK, :, 128:].reshape(NBLK * VPT, 128),
                recvs[1 : NBLK + 1].reshape(NBLK * VPT, SLAB),
                recvs[2 : NBLK + 2, :, :128].reshape(NBLK * VPT, 128),
            ],
            1,
        )
        y = nt(w, tt[...])
        ysrc[...] = y.astype(BF).reshape(NBLK, VPT, SLAB)
        sq = y * y
        sq = sq[:, :128] + sq[:, 128:]
        esrc[i] = jnp.sum(sq.reshape(NBLK, VPT, 128), 0)
        for d in range(1, NTM):
            energy(2, d, 1).start()

    def filter_channels(q):
        def body(g, acc):
            b = g * 4
            w = jnp.concatenate(
                [
                    recv[q, pl.ds(b, 4), :, 128:].reshape(4 * HALF, 128),
                    recv[q, pl.ds(b + 1, 4)].reshape(4 * HALF, SLAB),
                    recv[q, pl.ds(b + 2, 4), :, :128].reshape(4 * HALF, 128),
                ],
                1,
            )
            y = nt(w, tt[...])
            ybuf[pl.ds(b, 4)] = y.astype(BF).reshape(4, HALF, SLAB)
            sq = y * y
            sq = sq[:, :128] + sq[:, 128:]
            return acc + jnp.sum(sq.reshape(4, HALF, 128), 0)

        acc = lax.fori_loop(0, NBLK // 4, body, jnp.zeros((HALF, 128), F32))
        ebuf[q, i] = jnp.sum(acc.T.reshape(16, 8, HALF), 0)
        for d in range(1, NTM):
            energy(q, d, 1).start()

    def limit(total):
        return 2.0 * jnp.sqrt(total / T_ALL + 1e-6)

    def source_copy(e):
        return pltpu.make_async_remote_copy(
            src_ref=sp_out, dst_ref=sg.at[i], send_sem=s_send.at[e], recv_sem=s_recv.at[i],
            device_id=(group, base + e), device_id_type=MESH,
        )

    def source_landed(t):
        return pltpu.make_async_remote_copy(
            src_ref=sp_out, dst_ref=sg.at[t], send_sem=s_send.at[0], recv_sem=s_recv.at[t],
            device_id=(t, base + i), device_id_type=MESH,
        )

    def whiten_sources():
        for d in range(1, NTM):
            energy(2, d, -1).wait_recv()
        total = esrc[0] + esrc[1] + esrc[2] + esrc[3]
        top = limit(jnp.sum(total, 1, keepdims=True))
        top = jnp.broadcast_to(top[None], (SEGS, VPT, 1)).reshape(SEGS * VPT, 1)
        parts = []
        for j in range(4):
            y = jnp.concatenate([ysrc[s * 4 + j] for s in range(SEGS)], 0).astype(F32)
            parts.append(jnp.clip(y, -top, top).astype(BF))
        sp = nt(jnp.concatenate(parts, 1), fwd[...])
        re, im = sp[:, :NB], sp[:, NB:]
        g = nt((re * re + im * im).astype(BF), grow[...])
        scale = lax.rsqrt(g[:, :NB] * rrow[0:1, :] + g[:, NB:] * (0.1 / NB) + 1e-6)
        white = jnp.concatenate([re * scale, im * scale], 1).astype(BF)
        sp_out[...] = white.reshape(SEGS, VPT, 2 * NB)
        for e in range(NTM):

            @pl.when((group != i) | (group != e))
            def _():
                source_copy(e).start()

        @pl.when(group == i)
        def _():
            sg[i] = sp_out[...]

    def sources_in():
        for t in range(NTM):

            @pl.when((i != t) | (group != i))
            def _():
                source_landed(t).wait_recv()

        flat = sg[...].reshape(NTM * SEGS * VPT, 2 * NB).astype(F32)
        smat[0] = flat[:, :NB]
        smat[1] = flat[:, NB:]

        def body(w, carry):
            re = smat[0, pl.ds(w, NTM * SEGS, stride=VPT), :]
            im = smat[1, pl.ds(w, NTM * SEGS, stride=VPT), :]
            real, imag = [], []
            for t in range(NTM):
                r, m = re[t * SEGS : (t + 1) * SEGS], im[t * SEGS : (t + 1) * SEGS]
                real += [r, m]
                imag += [-m, r]
            both = jnp.concatenate(real + imag, 0).T
            u[pl.ds(pl.multiple_of(2 * w * NB, NB), NB), 0:64] = both[:, :64]
            u[pl.ds(pl.multiple_of((2 * w + 1) * NB, NB), NB), 0:64] = both[:, 64:]
            return carry

        lax.fori_loop(0, VPT, body, 0)

    def whiten_channels(q):
        for d in range(1, NTM):
            energy(q, d, -1).wait_recv()
        total = ebuf[q, 0] + ebuf[q, 1] + ebuf[q, 2] + ebuf[q, 3]
        top = limit(jnp.sum(total, 0, keepdims=True))
        top = jnp.broadcast_to(top, (HALF, HALF)).T
        top = jnp.concatenate([top, top], 1)

        def body(s, carry):
            parts = []
            for j in range(4):
                y = ybuf[s * 4 + j].astype(F32)
                parts.append(jnp.clip(y, -top, top).astype(BF))
            sp = nt(fwd[...], jnp.concatenate(parts, 1))
            re, im = sp[:NB], sp[NB:]
            g = nn(grow[...], (re * re + im * im).astype(BF))
            scale = lax.rsqrt(g[:NB] * rcol[...] + g[NB:] * (0.1 / NB) + 1e-6)
            pbuf[pl.ds(s, NB, stride=16), :] = re * scale
            pbuf[pl.ds(8 + s, NB, stride=16), :] = im * scale
            return carry

        lax.fori_loop(0, SEGS, body, 0)
        zp[q] = pbuf[...].reshape(NB, 16, HALF).astype(BF)
        spread(q)

    def cross(q):
        def body(g, carry):
            for j in range(8):
                k = g * 8 + j
                lhs = u[pl.ds(k, 2 * VPT, stride=NB), :][:, :64].astype(BF)
                x[pl.ds(k, 2 * VPT, stride=NB), :] = nn(lhs, z[k, :, q * HALF : (q + 1) * HALF])
            return carry

        lax.fori_loop(0, NB // 8, body, 0)
        xout[:, :, q * HALF : (q + 1) * HALF] = x[...].reshape(VPT, 2 * NB, HALF).astype(BF)

    send_channels(0)
    arrive(2)
    halos_in(2)
    filter_sources()
    send_channels(1)
    whiten_sources()
    arrive(0)
    halos_in(0)
    filter_channels(0)
    whiten_channels(0)
    pass_on(0)
    arrive(1)
    halos_in(1)
    filter_channels(1)
    whiten_channels(1)
    sources_in()
    collect(0)
    pass_on(1)
    cross(0)
    collect(1)
    cross(1)

    for q in range(3):
        for d in range(1, NTM):
            energy(q, d, 1).wait_send()

        @pl.when(i < NTM - 1)
        def _():
            halo(q, 0).wait_send()

        @pl.when(i > 0)
        def _():
            halo(q, 1).wait_send()

        if q < 2:
            for h in range(2):
                direct(q, h, 0).wait_send()
                direct(q, h, 1).wait_send()
                forward(q, h).wait_send()
        if q > 0:

            def sent(d, carry, q=q):
                a2a(q, d, 1).wait_send()
                return carry

            lax.fori_loop(1, NBLK, sent, 0)

    for e in range(NTM):

        @pl.when((group != i) | (group != e))
        def _():
            source_copy(e).wait_send()


def cross_spectra(order, vs, raw, taps, fwd, grow, rcol, rrow):
    vm = pl.BlockSpec(memory_space=pltpu.VMEM)
    sm = pl.BlockSpec(memory_space=pltpu.SMEM)
    dma = pltpu.SemaphoreType.DMA
    return pl.pallas_call(
        spectra_kernel,
        out_shape=jax.ShapeDtypeStruct((VPT, 2 * NB, SLAB), BF),
        in_specs=[sm, sm, pl.BlockSpec(memory_space=pl.ANY), vm, vm, vm, vm, vm],
        out_specs=vm,
        scratch_shapes=[
            pltpu.VMEM((raw.shape[0], 2, 128), F32),
            pltpu.VMEM((2 * HALF, 128), F32),
            pltpu.VMEM((2, NBLK, HALF, SLAB), BF),
            pltpu.VMEM((VS, SLAB), BF),
            pltpu.VMEM((2, NBLK + 2, HALF, SLAB), BF),
            pltpu.VMEM((NBLK + 2, VPT, SLAB), BF),
            pltpu.VMEM((SLAB, 2 * SLAB), BF),
            pltpu.VMEM((NBLK, HALF, SLAB), BF),
            pltpu.VMEM((NBLK, VPT, SLAB), BF),
            pltpu.VMEM((NB * 16, HALF), F32),
            pltpu.VMEM((2, NB, 16, HALF), BF),
            pltpu.VMEM((NB, NTM * 16, SLAB), BF),
            pltpu.VMEM((SEGS, VPT, 2 * NB), BF),
            pltpu.VMEM((NTM, SEGS, VPT, 2 * NB), BF),
            pltpu.VMEM((2, NTM * SEGS * VPT, NB), F32),
            pltpu.VMEM((2 * VPT * NB, 128), F32),
            pltpu.VMEM((2 * VPT * NB, HALF), F32),
            pltpu.VMEM((2, NTM, 8, HALF), F32),
            pltpu.VMEM((NTM, VPT, 128), F32),
            dma((8,)), dma((3, NBLK)), dma((3, NBLK)), dma((3, 2)), dma((3, 2)),
            dma((3, NTM)), dma((3, NTM)), dma((2, 2, 3)), dma((2, 2, NTM)),
            dma((NTM,)), dma((NTM,)),
        ],
        compiler_params=pltpu.CompilerParams(
            collective_id=0, has_side_effects=True, vmem_limit_bytes=50 * MIB
        ),
    )(order, vs, raw, taps, fwd, grow, rcol, rrow)


def lag_kernel(x, inv, out):
    out[0] = tn(x[0], inv[...])


def lags(x, inv):
    return pl.pallas_call(
        lag_kernel,
        grid=(VPT,),
        in_specs=[
            pl.BlockSpec((1, 2 * NB, SLAB), lambda v: (v, 0, 0)),
            pl.BlockSpec((2 * NB, NF), lambda v: (0, 0)),
        ],
        out_specs=pl.BlockSpec((1, SLAB, NF), lambda v: (v, 0, 0)),
        out_shape=jax.ShapeDtypeStruct((VPT, SLAB, NF), F32),
        compiler_params=pltpu.CompilerParams(vmem_limit_bytes=32 * MIB),
    )(x, inv)


def on_device(raw_traces, fir_taps, chan_order, vs_index):
    fwd, inv, grow, rcount = tables()
    taps = jnp.broadcast_to(jnp.pad(fir_taps, (64, 2 * SLAB - 64 - TAPS))[None, :], (8, 2 * SLAB))
    x = cross_spectra(
        chan_order, vs_index, raw_traces, taps,
        jnp.asarray(fwd, BF), jnp.asarray(grow, BF),
        jnp.asarray(np.broadcast_to(rcount[:, None], (NB, HALF))),
        jnp.asarray(np.broadcast_to(rcount[None, :], (8, NB))),
    )
    return lags(x, jnp.asarray(inv, BF))


def solution(mesh):
    in_specs = (P(None, ("tm", "chan")), P(), P(), P())
    out_specs = P("tm", "chan", None)
    return jax.shard_map(
        on_device, mesh=mesh, in_specs=in_specs, out_specs=out_specs, check_vma=False
    )
```

```python
import functools
import math

import jax
import jax.numpy as jnp
import numpy as np
from jax import lax
from jax.experimental import pallas as pl
from jax.experimental.pallas import tpu as pltpu
from jax.sharding import PartitionSpec as P

NF = 1024
NB = 128
K0 = 4
WS = 8
TAPS = 129
SLAB = 256
NBLK = 32
NTM = 4
SEGS = 8
VS = 64
VPT = VS // NTM
CHUNK = 64
QN = SLAB // CHUNK
HB = NB // 2
T_ALL = SLAB * NBLK * NTM
MIB = 1024 * 1024
MESH = pl.DeviceIdType.MESH
BF = jnp.bfloat16
F32 = jnp.float32


def tables():
    k = np.arange(NB, dtype=np.int64)[:, None] + K0
    n = np.arange(NF, dtype=np.int64)[None, :]
    ph = (k * n % NF) * (2.0 * math.pi / NF)
    fwd = np.concatenate([np.cos(ph), -np.sin(ph)], 0) / math.sqrt(NF)
    lag = (k * (n - NF // 2) % NF) * (2.0 * math.pi / NF)
    inv = np.concatenate([np.cos(lag), -np.sin(lag)], 0) / math.sqrt(SEGS * NTM * NB)
    near = np.abs(np.arange(NB)[:, None] - np.arange(NB)[None, :]) <= WS
    grow = np.concatenate([near, np.ones((NB, NB))], 0)
    return (
        fwd.astype(np.float32),
        inv.astype(np.float32),
        grow.astype(np.float32),
    )


def nt(a, b):
    return lax.dot_general(a, b, (((1,), (1,)), ((), ())), preferred_element_type=F32)


def tn(a, b):
    return lax.dot_general(a, b, (((0,), (0,)), ((), ())), preferred_element_type=F32)


def nn(a, b):
    return jnp.dot(a, b, preferred_element_type=F32)


def spectra_kernel(
    order_in, vs_in, raw, taps_in, fwd_in, grow_in, xout,
    order, vs, taps, fwd, grow, xs, rows2, line, send, srcs, recv, recvs, tt, ybuf, ysrc, pbuf, zp, z, sp_out, sg, smat, u, x,
    ebuf, esrc, r_sem, a_send, a_recv, h_send, h_recv, e_send, e_recv, g_send, g_recv,
    s_send, s_recv, x_sem,
):
    i = lax.axis_index("tm")
    c = lax.axis_index("chan")
    cz, cx, cc = c // 8, (c // 2) % 4, c % 2
    group, base = c % NTM, (c // NTM) * NTM
    up, down = lax.rem(i + 1, NTM), lax.rem(i + NTM - 1, NTM)

    def at_shift(d, sign):
        d = (d * 11) % NBLK
        z = lax.rem(cz + sign * (d // 8) + 4, 4)
        x = lax.rem(cx + sign * ((d // 2) % 4) + 4, 4)
        k = lax.rem(cc + d % 2, 2)
        return z * 8 + x * 2 + k

    def load(p):
        part = raw.shape[0] // 4
        r = pl.ds((p // 2) * part, part)
        return pltpu.make_async_copy(
            raw.at[r, pl.ds((p % 2) * 128, 128)], rows2.at[r, p % 2], r_sem.at[p]
        )

    small = [
        pltpu.make_async_copy(a, b, r_sem.at[8 + n])
        for n, (a, b) in enumerate(
            (
                (taps_in, taps), (order_in, order), (vs_in, vs), (fwd_in, fwd), (grow_in, grow),
            )
        )
    ]
    for copy in small:
        copy.start()
    for p in range(8):
        load(p).start()

    barrier = pltpu.get_barrier_semaphore()

    def greet(d, carry):
        pl.semaphore_signal(barrier, inc=1, device_id=(i, at_shift(d, 1)), device_id_type=MESH)
        return carry

    lax.fori_loop(1, NBLK, greet, 0)
    for d in range(1, NTM):
        pl.semaphore_signal(
            barrier, inc=1, device_id=(lax.rem(i + d, NTM), c), device_id_type=MESH
        )
    for t in range(NTM):

        @pl.when((i != t) | (group != i))
        def _():
            pl.semaphore_signal(barrier, inc=1, device_id=(t, base + i), device_id_type=MESH)

    for copy in small:
        copy.wait()
    lane = lax.broadcasted_iota(jnp.int32, (1, 2 * SLAB), 1)

    def tap(j, row):
        return jnp.where(lane == j + 64, taps[j], row)

    band = lax.fori_loop(0, TAPS, tap, jnp.zeros((1, 2 * SLAB), F32))
    band = jnp.broadcast_to(band, (SLAB, 2 * SLAB))
    tt[...] = pltpu.roll(band, 0, 1, stride=1, stride_axis=0).astype(BF)

    for p in range(8):
        load(p).wait()
    peers = NBLK - 1 + NTM - 1 + NTM

    @pl.when(group == i)
    def _():
        pl.semaphore_wait(barrier, peers - 1)

    @pl.when(group != i)
    def _():
        pl.semaphore_wait(barrier, peers)

    def a2a(q, d, sign):
        other = at_shift(d, sign)
        owner = c if sign > 0 else other
        if q == QN:
            src, dst = srcs.at[pl.ds((other % NTM) * VPT, VPT)], recvs.at[1 + owner]
        else:
            src, dst = send.at[q, d], recv.at[q, 1 + owner]
        return pltpu.make_async_remote_copy(
            src_ref=src, dst_ref=dst, send_sem=a_send.at[q, d], recv_sem=a_recv.at[q, owner],
            device_id=(i, other), device_id_type=MESH,
        )

    def fetch(count, position):
        def body(g, carry):
            for t in range(64):
                r = g * 64 + t
                line[pl.ds(pl.multiple_of(2 * r, 2), 2), :] = rows2[position(r)]
            return carry

        lax.fori_loop(0, count // 64, body, 0)
        return [line[pl.ds(h, count, stride=2), :].astype(BF) for h in range(2)]

    lo, hi = fetch(VS, lambda r: order[vs[r]])
    srcs[:, 0:128] = lo
    srcs[:, 128:256] = hi

    def send_sources(d, carry):
        a2a(QN, d, 1).start()
        return carry

    lax.fori_loop(1, NBLK, send_sources, 0)
    recvs[1 + c] = srcs[pl.ds(pl.multiple_of(group * VPT, VPT), VPT)]

    def stage(q):
        lo, hi = fetch(CHUNK, lambda r: order[c * SLAB + q * CHUNK + r])
        recv[q, 1 + c, :, 0:128] = lo
        recv[q, 1 + c, :, 128:256] = hi

        def body(d, carry):
            first = at_shift(d, 1) * SLAB + q * CHUNK
            lo, hi = fetch(CHUNK, lambda r: order[first + r])
            send[q, d, :, 0:128] = lo
            send[q, d, :, 128:256] = hi
            if q == 0:
                a2a(q, d, 1).start()
            return carry

        lax.fori_loop(1, NBLK, body, 0)

    def send_channels(q, wait):
        def body(d, carry):
            if wait:
                a2a(q - 1, d, 1).wait_send()
            a2a(q, d, 1).start()
            return carry

        lax.fori_loop(1, NBLK, body, 0)

    def box(q):
        return recvs if q == QN else recv.at[q]

    def halo(q, side):
        b = box(q)
        if side == 0:
            return pltpu.make_async_remote_copy(
                src_ref=b.at[NBLK, :, pl.ds(128, 128)], dst_ref=b.at[0, :, pl.ds(128, 128)],
                send_sem=h_send.at[q, 0], recv_sem=h_recv.at[q, 0],
                device_id=(up, c), device_id_type=MESH,
            )
        return pltpu.make_async_remote_copy(
            src_ref=b.at[1, :, pl.ds(0, 128)], dst_ref=b.at[NBLK + 1, :, pl.ds(0, 128)],
            send_sem=h_send.at[q, 1], recv_sem=h_recv.at[q, 1],
            device_id=(down, c), device_id_type=MESH,
        )

    def arrive(q):
        def wait(d, carry):
            a2a(q, d, -1).wait_recv()
            return carry

        lax.fori_loop(1, NBLK, wait, 0)
        b = box(q)
        rows = VPT if q == QN else CHUNK

        @pl.when(i < NTM - 1)
        def _():
            halo(q, 0).start()

        @pl.when(i > 0)
        def _():
            halo(q, 1).start()

        @pl.when(i == 0)
        def _():
            b[0, :, pl.ds(128, 128)] = jnp.zeros((rows, 128), BF)

        @pl.when(i == NTM - 1)
        def _():
            b[NBLK + 1, :, pl.ds(0, 128)] = jnp.zeros((rows, 128), BF)

    def halos_in(q):
        @pl.when(i > 0)
        def _():
            halo(q, 0).wait_recv()

        @pl.when(i < NTM - 1)
        def _():
            halo(q, 1).wait_recv()

    def energy(q, d, sign):
        other = lax.rem(i + d, NTM)
        owner = i if sign > 0 else other
        e = esrc if q == QN else ebuf.at[q]
        return pltpu.make_async_remote_copy(
            src_ref=e.at[owner], dst_ref=e.at[owner], send_sem=e_send.at[q, d],
            recv_sem=e_recv.at[q, owner], device_id=(other, c), device_id_type=MESH,
        )

    def block(q, h, owner):
        return z.at[q, pl.ds(h * 32, 32), pl.ds(owner * 16, 16)]

    def direct(q, h, way):
        return pltpu.make_async_remote_copy(
            src_ref=zp.at[q, pl.ds(h * 32, 32)], dst_ref=block(q, h, i),
            send_sem=g_send.at[q, h, way], recv_sem=g_recv.at[q, h, i],
            device_id=(up if way == 0 else down, c), device_id_type=MESH,
        )

    def forward(q, h):
        owner = down if h == 0 else up
        return pltpu.make_async_remote_copy(
            src_ref=block(q, h, owner), dst_ref=block(q, h, owner),
            send_sem=g_send.at[q, h, 2], recv_sem=g_recv.at[q, h, owner],
            device_id=(up if h == 0 else down, c), device_id_type=MESH,
        )

    def landed(q, h, owner):
        return pltpu.make_async_remote_copy(
            src_ref=block(q, h, owner), dst_ref=block(q, h, owner),
            send_sem=g_send.at[q, h, 2], recv_sem=g_recv.at[q, h, owner],
            device_id=(up, c), device_id_type=MESH,
        )

    def spread(q):
        for h in range(2):
            direct(q, h, h).start()
        for h in range(2):
            direct(q, h, 1 - h).start()
        z[q, :, pl.ds(pl.multiple_of(i * 16, 16), 16)] = zp[q]

    def pass_on(q):
        for h in range(2):
            landed(q, h, down if h == 0 else up).wait_recv()
            forward(q, h).start()

    def collect(q):
        for h in range(2):
            landed(q, h, up if h == 0 else down).wait_recv()
            landed(q, h, lax.rem(i + 2, NTM)).wait_recv()

    def filter_sources():
        w = jnp.concatenate(
            [
                recvs[0:NBLK, :, 128:].reshape(NBLK * VPT, 128),
                recvs[1 : NBLK + 1].reshape(NBLK * VPT, SLAB),
                recvs[2 : NBLK + 2, :, :128].reshape(NBLK * VPT, 128),
            ],
            1,
        )
        y = nt(w, tt[...])
        ysrc[...] = y.astype(BF).reshape(NBLK, VPT, SLAB)
        sq = y * y
        sq = sq[:, :128] + sq[:, 128:]
        esrc[i] = jnp.sum(sq.reshape(NBLK, VPT, 128), 0)
        for d in range(1, NTM):
            energy(QN, d, 1).start()

    def filter_channels(q):
        def body(g, acc):
            b = g * 8
            w = jnp.concatenate(
                [
                    recv[q, pl.ds(b, 8), :, 128:].reshape(8 * CHUNK, 128),
                    recv[q, pl.ds(b + 1, 8)].reshape(8 * CHUNK, SLAB),
                    recv[q, pl.ds(b + 2, 8), :, :128].reshape(8 * CHUNK, 128),
                ],
                1,
            )
            y = nt(w, tt[...])
            ybuf[pl.ds(b, 8)] = y.astype(BF).reshape(8, CHUNK, SLAB)
            sq = y * y
            sq = sq[:, :128] + sq[:, 128:]
            return acc + jnp.sum(sq.reshape(8, CHUNK, 128), 0)

        acc = lax.fori_loop(0, NBLK // 8, body, jnp.zeros((CHUNK, 128), F32))
        ebuf[q, i] = jnp.sum(jnp.concatenate([acc, acc], 0).T.reshape(16, 8, 2 * CHUNK), 0)
        for d in range(1, NTM):
            energy(q, d, 1).start()

    def limit(total):
        return 2.0 * jnp.sqrt(total / T_ALL + 1e-6)

    def source_copy(e):
        return pltpu.make_async_remote_copy(
            src_ref=sp_out, dst_ref=sg.at[i], send_sem=s_send.at[e], recv_sem=s_recv.at[i],
            device_id=(group, base + e), device_id_type=MESH,
        )

    def source_landed(t):
        return pltpu.make_async_remote_copy(
            src_ref=sp_out, dst_ref=sg.at[t], send_sem=s_send.at[0], recv_sem=s_recv.at[t],
            device_id=(t, base + i), device_id_type=MESH,
        )

    def per_bin(axis):
        k = lax.broadcasted_iota(jnp.int32, (NB, NB) if axis == 0 else (8, NB), axis)
        count = jnp.minimum(k + WS, NB - 1) - jnp.maximum(k - WS, 0) + 1
        inverse_count = 1.0 / count.astype(F32)
        return inverse_count if axis == 0 else inverse_count[0:1, :]

    def whiten_sources():
        for d in range(1, NTM):
            energy(QN, d, -1).wait_recv()
        total = esrc[0] + esrc[1] + esrc[2] + esrc[3]
        top = limit(jnp.sum(total, 1, keepdims=True))
        top = jnp.broadcast_to(top[None], (SEGS, VPT, 1)).reshape(SEGS * VPT, 1)
        parts = []
        for j in range(4):
            y = jnp.concatenate([ysrc[s * 4 + j] for s in range(SEGS)], 0).astype(F32)
            parts.append(jnp.clip(y, -top, top).astype(BF))
        sp = nt(jnp.concatenate(parts, 1), fwd[...])
        re, im = sp[:, :NB], sp[:, NB:]
        g = nt((re * re + im * im).astype(BF), grow[...])
        scale = lax.rsqrt(g[:, :NB] * per_bin(1) + g[:, NB:] * (0.1 / NB) + 1e-6)
        white = jnp.concatenate([re * scale, im * scale], 1).astype(BF)
        sp_out[...] = white.reshape(SEGS, VPT, 2 * NB)
        for e in range(NTM):

            @pl.when((group != i) | (group != e))
            def _():
                source_copy(e).start()

        @pl.when(group == i)
        def _():
            sg[i] = sp_out[...]

    def sources_in():
        for t in range(NTM):

            @pl.when((i != t) | (group != i))
            def _():
                source_landed(t).wait_recv()

        flat = sg[...].reshape(NTM * SEGS * VPT, 2 * NB).astype(F32)
        smat[0] = flat[:, :NB]
        smat[1] = flat[:, NB:]

        def body(w, carry):
            re = smat[0, pl.ds(w, NTM * SEGS, stride=VPT), :]
            im = smat[1, pl.ds(w, NTM * SEGS, stride=VPT), :]
            real, imag = [], []
            for t in range(NTM):
                r, m = re[t * SEGS : (t + 1) * SEGS], im[t * SEGS : (t + 1) * SEGS]
                real += [r, m]
                imag += [-m, r]
            both = jnp.concatenate(real + imag, 0).T
            u[pl.ds(pl.multiple_of(2 * w * NB, NB), NB), 0:64] = both[:, :64]
            u[pl.ds(pl.multiple_of((2 * w + 1) * NB, NB), NB), 0:64] = both[:, 64:]
            return carry

        lax.fori_loop(0, VPT, body, 0, unroll=4)

    def whiten_channels(q):
        for d in range(1, NTM):
            energy(q, d, -1).wait_recv()
        total = ebuf[q, 0] + ebuf[q, 1] + ebuf[q, 2] + ebuf[q, 3]
        top = limit(jnp.sum(total, 0, keepdims=True))
        top = jnp.broadcast_to(top, (128, 128)).T[0:CHUNK]
        top = jnp.concatenate([top, top], 1)
        low = lax.broadcasted_iota(jnp.int32, (HB, 128), 1) < CHUNK

        def body(t, carry):
            parts = []
            for j in range(4):
                two = []
                for s in range(2):
                    y = ybuf[(2 * t + s) * 4 + j].astype(F32)
                    two.append(jnp.clip(y, -top, top).astype(BF))
                parts.append(jnp.concatenate(two, 0))
            sp = nt(fwd[...], jnp.concatenate(parts, 1))
            re, im = sp[:NB], sp[NB:]
            g = nn(grow[...], (re * re + im * im).astype(BF))
            scale = lax.rsqrt(g[:NB] * per_bin(0) + g[NB:] * (0.1 / NB) + 1e-6)
            for n, part in enumerate((re * scale, im * scale)):
                turned = pltpu.roll(part, CHUNK, 1)
                first = jnp.where(low, part[:HB], turned[HB:])
                second = jnp.where(low, turned[:HB], part[HB:])
                pbuf[pl.ds(n * SEGS + 2 * t, HB, stride=16), :] = first
                pbuf[pl.ds(n * SEGS + 2 * t + 1, HB, stride=16), :] = second
            return carry

        lax.fori_loop(0, SEGS // 2, body, 0, unroll=2)
        zp[q] = pbuf[...].reshape(HB, 16, 128).astype(BF)
        spread(q)

    def cross(q):
        def body(g, carry):
            for j in range(16):
                k = g * 16 + j
                lhs = u[pl.ds(k, 4 * VPT, stride=HB), :][:, :64].astype(BF)
                x[q % 2, pl.ds(k, 4 * VPT, stride=HB), :] = nn(lhs, z[q, k])
            return carry

        lax.fori_loop(0, HB // 16, body, 0)

    def leave(p, g):
        part = pl.ds(2 * g, 2)
        return pltpu.make_async_copy(xs.at[p, part], xout.at[p, part], x_sem.at[p, g])

    def merge(p):
        low = lax.broadcasted_iota(jnp.int32, (HB, 128), 1) < CHUNK

        def body(g, carry):
            done = []
            for t in range(4):
                for kh in range(2):
                    rows = pl.ds(pl.multiple_of(g * (4 * NB) + t * NB + kh * HB, HB), HB)
                    even, odd = x[0, rows, :], x[1, rows, :]
                    if kh == 0:
                        both = jnp.where(low, even, pltpu.roll(odd, CHUNK, 1))
                    else:
                        both = jnp.where(low, pltpu.roll(even, CHUNK, 1), odd)
                    done.append((t, kh, both.astype(BF)))
            for t, kh, both in done:
                k0 = (t % 2) * NB + kh * HB
                xs[p, 2 * g + t // 2, k0 : k0 + HB] = both
            leave(p, g).start()
            return carry

        lax.fori_loop(0, VPT // 2, body, 0)

    stage(0)
    arrive(QN)
    stage(1)
    send_channels(1, True)
    halos_in(QN)
    filter_sources()
    arrive(0)
    stage(2)
    whiten_sources()
    halos_in(0)
    filter_channels(0)
    sources_in()
    whiten_channels(0)
    send_channels(2, False)
    arrive(1)
    stage(3)
    halos_in(1)
    filter_channels(1)
    pass_on(0)
    whiten_channels(1)
    send_channels(3, False)
    arrive(2)
    collect(0)
    cross(0)
    halos_in(2)
    filter_channels(2)
    pass_on(1)
    whiten_channels(2)
    arrive(3)
    collect(1)
    cross(1)
    halos_in(3)
    filter_channels(3)
    pass_on(2)
    merge(0)
    whiten_channels(3)
    collect(2)
    cross(2)
    pass_on(3)
    collect(3)
    cross(3)
    merge(1)

    for p in range(2):
        for g in range(VPT // 2):
            leave(p, g).wait()
    for q in range(QN + 1):
        for d in range(1, NTM):
            energy(q, d, 1).wait_send()

        @pl.when(i < NTM - 1)
        def _():
            halo(q, 0).wait_send()

        @pl.when(i > 0)
        def _():
            halo(q, 1).wait_send()

        if q < QN:
            for h in range(2):
                direct(q, h, 0).wait_send()
                direct(q, h, 1).wait_send()
                forward(q, h).wait_send()
        if q > 0:

            def sent(d, carry, q=q):
                a2a(q, d, 1).wait_send()
                return carry

            lax.fori_loop(1, NBLK, sent, 0)

    for e in range(NTM):

        @pl.when((group != i) | (group != e))
        def _():
            source_copy(e).wait_send()


def cross_spectra(order, vs, raw, taps, fwd, grow):
    hb = pl.BlockSpec(memory_space=pl.ANY)
    dma = pltpu.SemaphoreType.DMA
    return pl.pallas_call(
        spectra_kernel,
        out_shape=jax.ShapeDtypeStruct((2, VPT, 2 * NB, 128), BF),
        in_specs=[hb] * 6,
        out_specs=hb,
        scratch_shapes=[
            pltpu.SMEM(order.shape, jnp.int32),
            pltpu.SMEM(vs.shape, jnp.int32),
            pltpu.SMEM(taps.shape, F32),
            pltpu.VMEM(fwd.shape, BF),
            pltpu.VMEM(grow.shape, BF),
            pltpu.VMEM((2, VPT, 2 * NB, 128), BF),
            pltpu.VMEM((raw.shape[0], 2, 128), F32),
            pltpu.VMEM((2 * CHUNK, 128), F32),
            pltpu.VMEM((QN, NBLK, CHUNK, SLAB), BF),
            pltpu.VMEM((VS, SLAB), BF),
            pltpu.VMEM((QN, NBLK + 2, CHUNK, SLAB), BF),
            pltpu.VMEM((NBLK + 2, VPT, SLAB), BF),
            pltpu.VMEM((SLAB, 2 * SLAB), BF),
            pltpu.VMEM((NBLK, CHUNK, SLAB), BF),
            pltpu.VMEM((NBLK, VPT, SLAB), BF),
            pltpu.VMEM((HB * 16, 128), F32),
            pltpu.VMEM((QN, HB, 16, 128), BF),
            pltpu.VMEM((QN, HB, NTM * 16, 128), BF),
            pltpu.VMEM((SEGS, VPT, 2 * NB), BF),
            pltpu.VMEM((NTM, SEGS, VPT, 2 * NB), BF),
            pltpu.VMEM((2, NTM * SEGS * VPT, NB), F32),
            pltpu.VMEM((2 * VPT * NB, 128), F32),
            pltpu.VMEM((2, 2 * VPT * NB, 128), F32),
            pltpu.VMEM((QN, NTM, 8, 128), F32),
            pltpu.VMEM((NTM, VPT, 128), F32),
            dma((13,)), dma((QN + 1, NBLK)), dma((QN + 1, NBLK)),
            dma((QN + 1, 2)), dma((QN + 1, 2)), dma((QN + 1, NTM)), dma((QN + 1, NTM)),
            dma((QN, 2, 3)), dma((QN, 2, NTM)), dma((NTM,)), dma((NTM,)), dma((2, VPT // 2)),
        ],
        compiler_params=pltpu.CompilerParams(
            collective_id=0, has_side_effects=True, vmem_limit_bytes=56 * MIB
        ),
    )(order, vs, raw, taps, fwd, grow)


SLOTS = 4


def lag_kernel(x, inv, out, xb, buf, in_sem, sem):
    def enter(v):
        return pltpu.make_async_copy(x.at[:, v], xb.at[:, v], in_sem.at[v])

    def leave(v):
        return pltpu.make_async_copy(buf.at[v % SLOTS], out.at[v], sem.at[v % SLOTS])

    for v in range(VPT):
        enter(v).start()
    for v in range(VPT):
        enter(v).wait()
        if v >= SLOTS:
            leave(v - SLOTS).wait()
        for h in range(2):
            rows = slice(h * 128, h * 128 + 128)
            buf[v % SLOTS, rows] = tn(xb[h, v], inv[...])
        leave(v).start()
    for v in range(VPT - SLOTS, VPT):
        leave(v).wait()


def lags(x, inv):
    return pl.pallas_call(
        lag_kernel,
        in_specs=[pl.BlockSpec(memory_space=pl.ANY), pl.BlockSpec(memory_space=pltpu.VMEM)],
        out_specs=pl.BlockSpec(memory_space=pl.ANY),
        out_shape=jax.ShapeDtypeStruct((VPT, SLAB, NF), F32),
        scratch_shapes=[
            pltpu.VMEM((2, VPT, 2 * NB, 128), BF),
            pltpu.VMEM((SLOTS, SLAB, NF), F32),
            pltpu.SemaphoreType.DMA((VPT,)),
            pltpu.SemaphoreType.DMA((SLOTS,)),
        ],
        compiler_params=pltpu.CompilerParams(vmem_limit_bytes=60 * MIB),
    )(x, inv)


def on_device(raw_traces, fir_taps, chan_order, vs_index):
    fwd, inv, grow = tables()
    x = cross_spectra(
        chan_order, vs_index, raw_traces, fir_taps,
        jnp.asarray(fwd, BF), jnp.asarray(grow, BF),
    )
    return lags(x, jnp.asarray(inv, BF))


def solution(mesh):
    in_specs = (P(None, ("tm", "chan")), P(), P(), P())
    out_specs = P("tm", "chan", None)
    return jax.shard_map(
        on_device, mesh=mesh, in_specs=in_specs, out_specs=out_specs, check_vma=False
    )
```

```python
import functools
import math

import jax
import jax.numpy as jnp
import numpy as np
from jax import lax
from jax.experimental import pallas as pl
from jax.experimental.pallas import tpu as pltpu
from jax.sharding import PartitionSpec as P

NF = 1024
NB = 128
K0 = 4
WS = 8
TAPS = 129
SLAB = 256
NBLK = 32
NTM = 4
SEGS = 8
VS = 64
VPT = VS // NTM
CHUNK = 64
QN = SLAB // CHUNK
HB = NB // 2
T_ALL = SLAB * NBLK * NTM
MIB = 1024 * 1024
MESH = pl.DeviceIdType.MESH
BF = jnp.bfloat16
F32 = jnp.float32


def tables():
    k = np.arange(NB, dtype=np.int64)[:, None] + K0
    n = np.arange(NF, dtype=np.int64)[None, :]
    ph = (k * n % NF) * (2.0 * math.pi / NF)
    fwd = np.concatenate([np.cos(ph), -np.sin(ph)], 0) / math.sqrt(NF)
    lag = (k * (n - NF // 2) % NF) * (2.0 * math.pi / NF)
    inv = np.concatenate([np.cos(lag), -np.sin(lag)], 0) / math.sqrt(SEGS * NTM * NB)
    near = np.abs(np.arange(NB)[:, None] - np.arange(NB)[None, :]) <= WS
    grow = np.concatenate([near, np.ones((NB, NB))], 0)
    return (
        fwd.astype(np.float32),
        inv.astype(np.float32),
        grow.astype(np.float32),
    )


def nt(a, b):
    return lax.dot_general(a, b, (((1,), (1,)), ((), ())), preferred_element_type=F32)


def tn(a, b):
    return lax.dot_general(a, b, (((0,), (0,)), ((), ())), preferred_element_type=F32)


def nn(a, b):
    return jnp.dot(a, b, preferred_element_type=F32)


def spectra_kernel(
    order_in, vs_in, raw, taps_in, fwd_in, grow_in, xout,
    order, vs, taps, fwd, grow, xs, rows2, line, send, srcs, recv, recvs, tt, ybuf, ysrc, pbuf, zp, z, sp_out, sg, smat, u, x,
    ebuf, esrc, r_sem, a_send, a_recv, h_send, h_recv, e_send, e_recv, g_send, g_recv,
    s_send, s_recv, x_sem,
):
    i = lax.axis_index("tm")
    c = lax.axis_index("chan")
    cz, cx, cc = c // 8, (c // 2) % 4, c % 2
    group, base = c % NTM, (c // NTM) * NTM
    up, down = lax.rem(i + 1, NTM), lax.rem(i + NTM - 1, NTM)

    def at_shift(d, sign):
        d = (d * 13) % NBLK
        z = lax.rem(cz + sign * (d // 8) + 4, 4)
        x = lax.rem(cx + sign * ((d // 2) % 4) + 4, 4)
        k = lax.rem(cc + d % 2, 2)
        return z * 8 + x * 2 + k

    def load(p):
        part = raw.shape[0] // 4
        r = pl.ds((p // 2) * part, part)
        return pltpu.make_async_copy(
            raw.at[r, pl.ds((p % 2) * 128, 128)], rows2.at[r, p % 2], r_sem.at[p]
        )

    small = [
        pltpu.make_async_copy(a, b, r_sem.at[8 + n])
        for n, (a, b) in enumerate(
            (
                (taps_in, taps), (order_in, order), (vs_in, vs), (fwd_in, fwd), (grow_in, grow),
            )
        )
    ]
    for copy in small:
        copy.start()
    for p in range(8):
        load(p).start()

    barrier = pltpu.get_barrier_semaphore()

    def greet(d, carry):
        pl.semaphore_signal(barrier, inc=1, device_id=(i, at_shift(d, 1)), device_id_type=MESH)
        return carry

    lax.fori_loop(1, NBLK, greet, 0)
    for d in range(1, NTM):
        pl.semaphore_signal(
            barrier, inc=1, device_id=(lax.rem(i + d, NTM), c), device_id_type=MESH
        )
    for t in range(NTM):

        @pl.when((i != t) | (group != i))
        def _():
            pl.semaphore_signal(barrier, inc=1, device_id=(t, base + i), device_id_type=MESH)

    for copy in small:
        copy.wait()
    lane = lax.broadcasted_iota(jnp.int32, (1, 2 * SLAB), 1)

    def tap(j, row):
        return jnp.where(lane == j + 64, taps[j], row)

    band = lax.fori_loop(0, TAPS, tap, jnp.zeros((1, 2 * SLAB), F32))
    band = jnp.broadcast_to(band, (SLAB, 2 * SLAB))
    tt[...] = pltpu.roll(band, 0, 1, stride=1, stride_axis=0).astype(BF)

    for p in range(8):
        load(p).wait()
    peers = NBLK - 1 + NTM - 1 + NTM

    @pl.when(group == i)
    def _():
        pl.semaphore_wait(barrier, peers - 1)

    @pl.when(group != i)
    def _():
        pl.semaphore_wait(barrier, peers)

    def a2a(q, d, sign):
        other = at_shift(d, sign)
        owner = c if sign > 0 else other
        if q == QN:
            src, dst = srcs.at[pl.ds((other % NTM) * VPT, VPT)], recvs.at[1 + owner]
        else:
            src, dst = send.at[q, d], recv.at[q, 1 + owner]
        return pltpu.make_async_remote_copy(
            src_ref=src, dst_ref=dst, send_sem=a_send.at[q, d], recv_sem=a_recv.at[q, owner],
            device_id=(i, other), device_id_type=MESH,
        )

    def fetch(count, position):
        def body(g, carry):
            for t in range(64):
                r = g * 64 + t
                line[pl.ds(pl.multiple_of(2 * r, 2), 2), :] = rows2[position(r)]
            return carry

        lax.fori_loop(0, count // 64, body, 0)
        return [line[pl.ds(h, count, stride=2), :].astype(BF) for h in range(2)]

    lo, hi = fetch(VS, lambda r: order[vs[r]])
    srcs[:, 0:128] = lo
    srcs[:, 128:256] = hi

    def send_sources(d, carry):
        a2a(QN, d, 1).start()
        return carry

    lax.fori_loop(1, NBLK, send_sources, 0)
    recvs[1 + c] = srcs[pl.ds(pl.multiple_of(group * VPT, VPT), VPT)]

    def stage(q):
        lo, hi = fetch(CHUNK, lambda r: order[c * SLAB + q * CHUNK + r])
        recv[q, 1 + c, :, 0:128] = lo
        recv[q, 1 + c, :, 128:256] = hi

        def body(d, carry):
            first = at_shift(d, 1) * SLAB + q * CHUNK
            lo, hi = fetch(CHUNK, lambda r: order[first + r])
            send[q, d, :, 0:128] = lo
            send[q, d, :, 128:256] = hi
            if q == 0:
                a2a(q, d, 1).start()
            return carry

        lax.fori_loop(1, NBLK, body, 0)

    def send_channels(q, first, stop):
        def body(d, carry):
            a2a(q - 1, d, 1).wait_send()
            a2a(q, d, 1).start()
            return carry

        lax.fori_loop(first, stop, body, 0)

    def box(q):
        return recvs if q == QN else recv.at[q]

    def halo(q, side):
        b = box(q)
        if side == 0:
            return pltpu.make_async_remote_copy(
                src_ref=b.at[NBLK, :, pl.ds(128, 128)], dst_ref=b.at[0, :, pl.ds(128, 128)],
                send_sem=h_send.at[q, 0], recv_sem=h_recv.at[q, 0],
                device_id=(up, c), device_id_type=MESH,
            )
        return pltpu.make_async_remote_copy(
            src_ref=b.at[1, :, pl.ds(0, 128)], dst_ref=b.at[NBLK + 1, :, pl.ds(0, 128)],
            send_sem=h_send.at[q, 1], recv_sem=h_recv.at[q, 1],
            device_id=(down, c), device_id_type=MESH,
        )

    def arrive(q):
        def wait(d, carry):
            a2a(q, d, -1).wait_recv()
            return carry

        lax.fori_loop(1, NBLK, wait, 0)
        b = box(q)
        rows = VPT if q == QN else CHUNK

        @pl.when(i < NTM - 1)
        def _():
            halo(q, 0).start()

        @pl.when(i > 0)
        def _():
            halo(q, 1).start()

        @pl.when(i == 0)
        def _():
            b[0, :, pl.ds(128, 128)] = jnp.zeros((rows, 128), BF)

        @pl.when(i == NTM - 1)
        def _():
            b[NBLK + 1, :, pl.ds(0, 128)] = jnp.zeros((rows, 128), BF)

    def halos_in(q):
        @pl.when(i > 0)
        def _():
            halo(q, 0).wait_recv()

        @pl.when(i < NTM - 1)
        def _():
            halo(q, 1).wait_recv()

    def energy(q, d, sign):
        other = lax.rem(i + d, NTM)
        owner = i if sign > 0 else other
        e = esrc if q == QN else ebuf.at[q]
        return pltpu.make_async_remote_copy(
            src_ref=e.at[owner], dst_ref=e.at[owner], send_sem=e_send.at[q, d],
            recv_sem=e_recv.at[q, owner], device_id=(other, c), device_id_type=MESH,
        )

    def block(q, h, owner):
        return z.at[q, pl.ds(h * 32, 32), pl.ds(owner * 16, 16)]

    def direct(q, h, way):
        return pltpu.make_async_remote_copy(
            src_ref=zp.at[q, pl.ds(h * 32, 32)], dst_ref=block(q, h, i),
            send_sem=g_send.at[q, h, way], recv_sem=g_recv.at[q, h, i],
            device_id=(up if way == 0 else down, c), device_id_type=MESH,
        )

    def forward(q, h):
        owner = down if h == 0 else up
        return pltpu.make_async_remote_copy(
            src_ref=block(q, h, owner), dst_ref=block(q, h, owner),
            send_sem=g_send.at[q, h, 2], recv_sem=g_recv.at[q, h, owner],
            device_id=(up if h == 0 else down, c), device_id_type=MESH,
        )

    def landed(q, h, owner):
        return pltpu.make_async_remote_copy(
            src_ref=block(q, h, owner), dst_ref=block(q, h, owner),
            send_sem=g_send.at[q, h, 2], recv_sem=g_recv.at[q, h, owner],
            device_id=(up, c), device_id_type=MESH,
        )

    def spread(q):
        for h in range(2):
            direct(q, h, h).start()
        for h in range(2):
            direct(q, h, 1 - h).start()
        z[q, :, pl.ds(pl.multiple_of(i * 16, 16), 16)] = zp[q]

    def pass_on(q):
        for h in range(2):
            landed(q, h, down if h == 0 else up).wait_recv()
            forward(q, h).start()

    def collect(q):
        for h in range(2):
            landed(q, h, up if h == 0 else down).wait_recv()
            landed(q, h, lax.rem(i + 2, NTM)).wait_recv()

    def filter_sources():
        w = jnp.concatenate(
            [
                recvs[0:NBLK, :, 128:].reshape(NBLK * VPT, 128),
                recvs[1 : NBLK + 1].reshape(NBLK * VPT, SLAB),
                recvs[2 : NBLK + 2, :, :128].reshape(NBLK * VPT, 128),
            ],
            1,
        )
        y = nt(w, tt[...])
        ysrc[...] = y.astype(BF).reshape(NBLK, VPT, SLAB)
        sq = y * y
        sq = sq[:, :128] + sq[:, 128:]
        esrc[i] = jnp.sum(sq.reshape(NBLK, VPT, 128), 0)
        for d in range(1, NTM):
            energy(QN, d, 1).start()

    def filter_channels(q):
        def body(g, acc):
            b = g * 8
            w = jnp.concatenate(
                [
                    recv[q, pl.ds(b, 8), :, 128:].reshape(8 * CHUNK, 128),
                    recv[q, pl.ds(b + 1, 8)].reshape(8 * CHUNK, SLAB),
                    recv[q, pl.ds(b + 2, 8), :, :128].reshape(8 * CHUNK, 128),
                ],
                1,
            )
            y = nt(w, tt[...])
            ybuf[pl.ds(b, 8)] = y.astype(BF).reshape(8, CHUNK, SLAB)
            sq = y * y
            sq = sq[:, :128] + sq[:, 128:]
            return acc + jnp.sum(sq.reshape(8, CHUNK, 128), 0)

        acc = lax.fori_loop(0, NBLK // 8, body, jnp.zeros((CHUNK, 128), F32))
        ebuf[q, i] = jnp.sum(jnp.concatenate([acc, acc], 0).T.reshape(16, 8, 2 * CHUNK), 0)
        for d in range(1, NTM):
            energy(q, d, 1).start()

    def limit(total):
        return 2.0 * jnp.sqrt(total / T_ALL + 1e-6)

    def source_copy(e):
        return pltpu.make_async_remote_copy(
            src_ref=sp_out, dst_ref=sg.at[i], send_sem=s_send.at[e], recv_sem=s_recv.at[i],
            device_id=(group, base + e), device_id_type=MESH,
        )

    def source_landed(t):
        return pltpu.make_async_remote_copy(
            src_ref=sp_out, dst_ref=sg.at[t], send_sem=s_send.at[0], recv_sem=s_recv.at[t],
            device_id=(t, base + i), device_id_type=MESH,
        )

    def per_bin(axis):
        k = lax.broadcasted_iota(jnp.int32, (NB, NB) if axis == 0 else (8, NB), axis)
        count = jnp.minimum(k + WS, NB - 1) - jnp.maximum(k - WS, 0) + 1
        inverse_count = 1.0 / count.astype(F32)
        return inverse_count if axis == 0 else inverse_count[0:1, :]

    def whiten_sources():
        for d in range(1, NTM):
            energy(QN, d, -1).wait_recv()
        total = esrc[0] + esrc[1] + esrc[2] + esrc[3]
        top = limit(jnp.sum(total, 1, keepdims=True))
        top = jnp.broadcast_to(top[None], (SEGS, VPT, 1)).reshape(SEGS * VPT, 1)
        parts = []
        for j in range(4):
            y = jnp.concatenate([ysrc[s * 4 + j] for s in range(SEGS)], 0).astype(F32)
            parts.append(jnp.clip(y, -top, top).astype(BF))
        sp = nt(jnp.concatenate(parts, 1), fwd[...])
        re, im = sp[:, :NB], sp[:, NB:]
        g = nt((re * re + im * im).astype(BF), grow[...])
        scale = lax.rsqrt(g[:, :NB] * per_bin(1) + g[:, NB:] * (0.1 / NB) + 1e-6)
        white = jnp.concatenate([re * scale, im * scale], 1).astype(BF)
        sp_out[...] = white.reshape(SEGS, VPT, 2 * NB)
        for e in range(NTM):

            @pl.when((group != i) | (group != e))
            def _():
                source_copy(e).start()

        @pl.when(group == i)
        def _():
            sg[i] = sp_out[...]

    def sources_in():
        for t in range(NTM):

            @pl.when((i != t) | (group != i))
            def _():
                source_landed(t).wait_recv()

        flat = sg[...].reshape(NTM * SEGS * VPT, 2 * NB).astype(F32)
        smat[0] = flat[:, :NB]
        smat[1] = flat[:, NB:]

        def body(w, carry):
            re = smat[0, pl.ds(w, NTM * SEGS, stride=VPT), :]
            im = smat[1, pl.ds(w, NTM * SEGS, stride=VPT), :]
            real, imag = [], []
            for t in range(NTM):
                r, m = re[t * SEGS : (t + 1) * SEGS], im[t * SEGS : (t + 1) * SEGS]
                real += [r, m]
                imag += [-m, r]
            both = jnp.concatenate(real + imag, 0).T
            u[pl.ds(pl.multiple_of(2 * w * NB, NB), NB), 0:64] = both[:, :64]
            u[pl.ds(pl.multiple_of((2 * w + 1) * NB, NB), NB), 0:64] = both[:, 64:]
            return carry

        lax.fori_loop(0, VPT, body, 0, unroll=4)

    def whiten_channels(q):
        for d in range(1, NTM):
            energy(q, d, -1).wait_recv()
        total = ebuf[q, 0] + ebuf[q, 1] + ebuf[q, 2] + ebuf[q, 3]
        top = limit(jnp.sum(total, 0, keepdims=True))
        top = jnp.broadcast_to(top, (128, 128)).T[0:CHUNK]
        top = jnp.concatenate([top, top], 1)
        low = lax.broadcasted_iota(jnp.int32, (HB, 128), 1) < CHUNK

        def body(t, carry):
            parts = []
            for j in range(4):
                two = []
                for s in range(2):
                    y = ybuf[(2 * t + s) * 4 + j].astype(F32)
                    two.append(jnp.clip(y, -top, top).astype(BF))
                parts.append(jnp.concatenate(two, 0))
            sp = nt(fwd[...], jnp.concatenate(parts, 1))
            re, im = sp[:NB], sp[NB:]
            g = nn(grow[...], (re * re + im * im).astype(BF))
            scale = lax.rsqrt(g[:NB] * per_bin(0) + g[NB:] * (0.1 / NB) + 1e-6)
            for n, part in enumerate((re * scale, im * scale)):
                turned = pltpu.roll(part, CHUNK, 1)
                first = jnp.where(low, part[:HB], turned[HB:])
                second = jnp.where(low, turned[:HB], part[HB:])
                pbuf[pl.ds(n * SEGS + 2 * t, HB, stride=16), :] = first
                pbuf[pl.ds(n * SEGS + 2 * t + 1, HB, stride=16), :] = second
            return carry

        lax.fori_loop(0, SEGS // 2, body, 0, unroll=2)
        zp[q] = pbuf[...].reshape(HB, 16, 128).astype(BF)
        spread(q)

    def cross(q):
        def body(g, carry):
            for j in range(16):
                k = g * 16 + j
                lhs = u[pl.ds(k, 4 * VPT, stride=HB), :][:, :64].astype(BF)
                x[q % 2, pl.ds(k, 4 * VPT, stride=HB), :] = nn(lhs, z[q, k])
            return carry

        lax.fori_loop(0, HB // 16, body, 0)

    def leave(p, g):
        part = pl.ds(2 * g, 2)
        return pltpu.make_async_copy(xs.at[p, part], xout.at[p, part], x_sem.at[p, g])

    def merge(p):
        low = lax.broadcasted_iota(jnp.int32, (HB, 128), 1) < CHUNK

        def body(g, carry):
            done = []
            for t in range(4):
                for kh in range(2):
                    rows = pl.ds(pl.multiple_of(g * (4 * NB) + t * NB + kh * HB, HB), HB)
                    even, odd = x[0, rows, :], x[1, rows, :]
                    if kh == 0:
                        both = jnp.where(low, even, pltpu.roll(odd, CHUNK, 1))
                    else:
                        both = jnp.where(low, pltpu.roll(even, CHUNK, 1), odd)
                    done.append((t, kh, both.astype(BF)))
            for t, kh, both in done:
                k0 = (t % 2) * NB + kh * HB
                xs[p, 2 * g + t // 2, k0 : k0 + HB] = both
            leave(p, g).start()
            return carry

        lax.fori_loop(0, VPT // 2, body, 0)

    stage(0)
    arrive(QN)
    stage(1)
    send_channels(1, 1, 16)
    halos_in(QN)
    filter_sources()
    send_channels(1, 16, NBLK)
    arrive(0)
    stage(2)
    send_channels(2, 1, 11)
    halos_in(0)
    filter_channels(0)
    send_channels(2, 11, 18)
    whiten_channels(0)
    send_channels(2, 18, 26)
    whiten_sources()
    send_channels(2, 26, NBLK)
    arrive(1)
    stage(3)
    send_channels(3, 1, 11)
    halos_in(1)
    filter_channels(1)
    pass_on(0)
    send_channels(3, 11, 18)
    whiten_channels(1)
    send_channels(3, 18, 26)
    sources_in()
    send_channels(3, 26, NBLK)
    arrive(2)
    collect(0)
    cross(0)
    halos_in(2)
    filter_channels(2)
    pass_on(1)
    whiten_channels(2)
    arrive(3)
    collect(1)
    cross(1)
    halos_in(3)
    filter_channels(3)
    pass_on(2)
    merge(0)
    whiten_channels(3)
    collect(2)
    cross(2)
    pass_on(3)
    collect(3)
    cross(3)
    merge(1)

    for p in range(2):
        for g in range(VPT // 2):
            leave(p, g).wait()
    for q in range(QN + 1):
        for d in range(1, NTM):
            energy(q, d, 1).wait_send()

        @pl.when(i < NTM - 1)
        def _():
            halo(q, 0).wait_send()

        @pl.when(i > 0)
        def _():
            halo(q, 1).wait_send()

        if q < QN:
            for h in range(2):
                direct(q, h, 0).wait_send()
                direct(q, h, 1).wait_send()
                forward(q, h).wait_send()
        if q >= QN - 1:

            def sent(d, carry, q=q):
                a2a(q, d, 1).wait_send()
                return carry

            lax.fori_loop(1, NBLK, sent, 0)

    for e in range(NTM):

        @pl.when((group != i) | (group != e))
        def _():
            source_copy(e).wait_send()


def cross_spectra(order, vs, raw, taps, fwd, grow):
    hb = pl.BlockSpec(memory_space=pl.ANY)
    dma = pltpu.SemaphoreType.DMA
    return pl.pallas_call(
        spectra_kernel,
        out_shape=jax.ShapeDtypeStruct((2, VPT, 2 * NB, 128), BF),
        in_specs=[hb] * 6,
        out_specs=hb,
        scratch_shapes=[
            pltpu.SMEM(order.shape, jnp.int32),
            pltpu.SMEM(vs.shape, jnp.int32),
            pltpu.SMEM(taps.shape, F32),
            pltpu.VMEM(fwd.shape, BF),
            pltpu.VMEM(grow.shape, BF),
            pltpu.VMEM((2, VPT, 2 * NB, 128), BF),
            pltpu.VMEM((raw.shape[0], 2, 128), F32),
            pltpu.VMEM((2 * CHUNK, 128), F32),
            pltpu.VMEM((QN, NBLK, CHUNK, SLAB), BF),
            pltpu.VMEM((VS, SLAB), BF),
            pltpu.VMEM((QN, NBLK + 2, CHUNK, SLAB), BF),
            pltpu.VMEM((NBLK + 2, VPT, SLAB), BF),
            pltpu.VMEM((SLAB, 2 * SLAB), BF),
            pltpu.VMEM((NBLK, CHUNK, SLAB), BF),
            pltpu.VMEM((NBLK, VPT, SLAB), BF),
            pltpu.VMEM((HB * 16, 128), F32),
            pltpu.VMEM((QN, HB, 16, 128), BF),
            pltpu.VMEM((QN, HB, NTM * 16, 128), BF),
            pltpu.VMEM((SEGS, VPT, 2 * NB), BF),
            pltpu.VMEM((NTM, SEGS, VPT, 2 * NB), BF),
            pltpu.VMEM((2, NTM * SEGS * VPT, NB), F32),
            pltpu.VMEM((2 * VPT * NB, 128), F32),
            pltpu.VMEM((2, 2 * VPT * NB, 128), F32),
            pltpu.VMEM((QN, NTM, 8, 128), F32),
            pltpu.VMEM((NTM, VPT, 128), F32),
            dma((13,)), dma((QN + 1, NBLK)), dma((QN + 1, NBLK)),
            dma((QN + 1, 2)), dma((QN + 1, 2)), dma((QN + 1, NTM)), dma((QN + 1, NTM)),
            dma((QN, 2, 3)), dma((QN, 2, NTM)), dma((NTM,)), dma((NTM,)), dma((2, VPT // 2)),
        ],
        compiler_params=pltpu.CompilerParams(
            collective_id=0, has_side_effects=True, vmem_limit_bytes=56 * MIB
        ),
    )(order, vs, raw, taps, fwd, grow)


SLOTS = 4


def lag_kernel(x, inv, out, xb, buf, in_sem, sem):
    def enter(v):
        return pltpu.make_async_copy(x.at[:, v], xb.at[:, v], in_sem.at[v])

    def leave(v):
        return pltpu.make_async_copy(buf.at[v % SLOTS], out.at[v], sem.at[v % SLOTS])

    for v in range(VPT):
        enter(v).start()
    for v in range(VPT):
        enter(v).wait()
        if v >= SLOTS:
            leave(v - SLOTS).wait()
        for h in range(2):
            rows = slice(h * 128, h * 128 + 128)
            buf[v % SLOTS, rows] = tn(xb[h, v], inv[...])
        leave(v).start()
    for v in range(VPT - SLOTS, VPT):
        leave(v).wait()


def lags(x, inv):
    return pl.pallas_call(
        lag_kernel,
        in_specs=[pl.BlockSpec(memory_space=pl.ANY), pl.BlockSpec(memory_space=pltpu.VMEM)],
        out_specs=pl.BlockSpec(memory_space=pl.ANY),
        out_shape=jax.ShapeDtypeStruct((VPT, SLAB, NF), F32),
        scratch_shapes=[
            pltpu.VMEM((2, VPT, 2 * NB, 128), BF),
            pltpu.VMEM((SLOTS, SLAB, NF), F32),
            pltpu.SemaphoreType.DMA((VPT,)),
            pltpu.SemaphoreType.DMA((SLOTS,)),
        ],
        compiler_params=pltpu.CompilerParams(vmem_limit_bytes=60 * MIB),
    )(x, inv)


def on_device(raw_traces, fir_taps, chan_order, vs_index):
    fwd, inv, grow = tables()
    x = cross_spectra(
        chan_order, vs_index, raw_traces, fir_taps,
        jnp.asarray(fwd, BF), jnp.asarray(grow, BF),
    )
    return lags(x, jnp.asarray(inv, BF))


def solution(mesh):
    in_specs = (P(None, ("tm", "chan")), P(), P(), P())
    out_specs = P("tm", "chan", None)
    return jax.shard_map(
        on_device, mesh=mesh, in_specs=in_specs, out_specs=out_specs, check_vma=False
    )
```
